512 devices in a mesh: rep: 4 (over x), ctx: 16 (over z, core), tp: 8 (over y).
Axes of the slice: x: 4, y: 8, z: 8, core: 2. Of those that a mesh axis runs over, the one named last changes fastest.
Arguments:
- q_arrived: bfloat16 [4, 6144, 4096], P('rep', 'ctx', 'tp'), may hold values from -6 to 6
- key_value_landed: bfloat16 [4, 6144, 2048], P('rep', 'ctx', 'tp'), may hold values from -6 to 6
- finish: int32 [48, 4], P('ctx'), may hold values from 0 to 3, as said below
- document_numbers: int32 [4, 6144], P('rep', 'ctx'), may hold values from 0 to 3, never falling along the last dimension, each value on 1 to 4608 neighbouring positions
Outputs:
- attended: bfloat16 [4, 6144, 4096], P('rep', 'ctx', 'tp')
The draws below stay inside these ranges and needn't reach their ends.
Inputs may be any that keep to these rules, and one draw needn't show every extreme that they name: `finish`: each row is a permutation of the scoring groups. Within the blocks of one index of ctx, taken in aligned runs of 4 blocks, no arrival group sends two blocks of a run to the same scoring group, so one arrival group sends one scoring group at most 1 block of one index of ctx.
All inputs are finite; a program needn't handle non-finite values.
Results may differ from the reference program's by a relative error of at most 0.0038.
Values may be sent and summed in bfloat16 or wider, within the bound.
A program may use at most 64 MiB of HBM per device.

```python
import math
import jax
import jax.numpy as jnp
import numpy as np
from jax import lax

QUERY_HEADS = 32
KEY_VALUE_HEADS = 8
HEAD_SIZE = 128
ARRIVAL_TOKENS = 128
TOK_DEV = 384
TRAJECTORY_LEN = 6144
NB = 48
N_REP = 4


def draw_q_arrived(key, part):
    key = jax.random.fold_in(key, 1)
    base_sample = jax.random.truncated_normal(key, -4.5, 4.5, (N_REP, TRAJECTORY_LEN, KEY_VALUE_HEADS, QUERY_HEADS // KEY_VALUE_HEADS, HEAD_SIZE))
    return base_sample.reshape(N_REP, TRAJECTORY_LEN, QUERY_HEADS * HEAD_SIZE).astype(jnp.bfloat16)


def draw_key_value_landed(key, part):
    key = jax.random.fold_in(key, 2)
    four_dim_shape = (N_REP, TRAJECTORY_LEN, KEY_VALUE_HEADS, HEAD_SIZE)
    key_draw = jax.random.truncated_normal(jax.random.fold_in(key, 1), -4.5, 4.5, four_dim_shape)
    value_draw = jax.random.truncated_normal(jax.random.fold_in(key, 2), -4.5, 4.5, four_dim_shape)
    stacked_rows = jnp.stack([key_draw, value_draw], axis=3)
    return stacked_rows.reshape(N_REP, TRAJECTORY_LEN, 2 * KEY_VALUE_HEADS * HEAD_SIZE).astype(jnp.bfloat16)


def draw_finish(key, part):
    key = jax.random.fold_in(key, 3)
    dev_blocks = TOK_DEV // ARRIVAL_TOKENS
    runs_dev = (dev_blocks + N_REP - 1) // N_REP
    block_num = jnp.arange(NB, dtype=jnp.int32)
    local_num = block_num % dev_blocks
    run_id = block_num // dev_blocks * runs_dev + local_num // N_REP
    inner = local_num % N_REP
    run_keys = jax.random.split(key, 3 * NB)
    permute = jax.vmap(lambda k: jax.random.permutation(k, N_REP).astype(jnp.int32))
    outer_perm = permute(run_keys[:NB])
    row_perm = permute(run_keys[NB:2 * NB])
    col_perm = permute(run_keys[2 * NB:])
    outer_rows = outer_perm[run_id]
    row_shift = jnp.take_along_axis(row_perm[run_id], inner[:, None], axis=1)
    col_shift = col_perm[run_id]
    latin = (row_shift + col_shift) % N_REP
    return jnp.take_along_axis(outer_rows, latin, axis=1).astype(jnp.int32)


def split_up(amount, total, bound, lean):
    portions = [(1 << 20) // math.isqrt(standing ** lean) + 1 for standing in range(2, amount + 1)]
    rest, given = total - bound - (amount - 1), [1] * (amount - 1)
    while rest > 0:
        candidates = [i for i in range(amount - 1) if given[i] < bound]
        pool, budget = sum([portions[i] for i in candidates]), rest
        for i in candidates:
            addition = min(bound - given[i], max(1, budget * portions[i] // pool), rest)
            given[i] = given[i] + addition
            rest = rest - addition
    return np.array([bound] + given)


def uneven_parts(key, amount, total, most, skew):
    if amount == 2:
        one = jax.random.randint(key, (), max(1, total - most), min(most, total - 1) + 1)
        return jnp.stack([one, total - one])
    lengths = jnp.asarray(split_up(amount, total, most, skew), jnp.int32)
    pairs = (amount - 1) // 2
    giver, sink = lengths[1:1 + 2 * pairs:2], lengths[2:2 + 2 * pairs:2]
    slack = jnp.minimum(giver - 1, most - sink)
    moved = jax.random.randint(jax.random.fold_in(key, 1), (pairs,), 0, 1 << 20) % (slack + 1)
    lengths = lengths.at[1:1 + 2 * pairs:2].set(giver - moved).at[2:2 + 2 * pairs:2].set(sink + moved)
    return lengths[jax.random.permutation(jax.random.fold_in(key, 2), amount)]


def setup_inputs(seed: int = 0) -> dict:
    key_list = jax.random.split(jax.random.key(seed), 5)
    return {
        "q_arrived": draw_q_arrived(jax.random.fold_in(key_list[4], 71), 0),
        "key_value_landed": draw_key_value_landed(jax.random.fold_in(key_list[4], 71), 0),
        "finish": draw_finish(jax.random.fold_in(key_list[4], 71), 0),
        "document_numbers": jax.vmap(lambda own: jnp.searchsorted(jnp.cumsum(uneven_parts(own, 4, TRAJECTORY_LEN, 3 * TRAJECTORY_LEN // 4, 0)), jnp.arange(TRAJECTORY_LEN), side="right"))(jax.random.split(key_list[3], N_REP)).reshape((N_REP, TRAJECTORY_LEN)).astype(jnp.int32),
    }


def score_tile(query_rows, key_tile):
    return jnp.einsum("gqd,kd->gqk", query_rows.astype(jnp.float32), key_tile.astype(jnp.float32)) * (query_rows.shape[-1] ** -0.5)


def visible_tile(query_pos, query_doc, key_pos, key_doc):
    return (key_pos[None, :] >= 0) & (key_pos[None, :] <= query_pos[:, None]) & (key_doc[None, :] == query_doc[:, None])


def attend(query_rows, key_cols, value_cols, query_pos, query_doc, key_pos, key_doc, tile_len):
    tiles = key_cols.shape[0] // tile_len

    def pieces(tile_num):
        offset = tile_num * tile_len
        return (lax.dynamic_slice_in_dim(key_cols, offset, tile_len, 0),
                lax.dynamic_slice_in_dim(value_cols, offset, tile_len, 0),
                lax.dynamic_slice_in_dim(key_pos, offset, tile_len, 0),
                lax.dynamic_slice_in_dim(key_doc, offset, tile_len, 0))

    def first_pass(tile_num, highest):
        key_tile, value_tile, pos_tile, doc_tile = pieces(tile_num)
        allowed = visible_tile(query_pos, query_doc, pos_tile, doc_tile)
        scores = jnp.where(allowed[None], score_tile(query_rows, key_tile), -1e30)
        return jnp.maximum(highest, jnp.max(scores, axis=-1))

    highest = lax.fori_loop(0, tiles, first_pass, jnp.full(query_rows.shape[:2], -1e30, jnp.float32))

    def second_pass(tile_num, state_pair):
        denom_sum, summed = state_pair
        key_tile, value_tile, pos_tile, doc_tile = pieces(tile_num)
        allowed = visible_tile(query_pos, query_doc, pos_tile, doc_tile)
        scores = score_tile(query_rows, key_tile)
        weights = jnp.where(allowed[None], jnp.exp(scores - highest[..., None]), 0.0)
        denom_sum = denom_sum + jnp.sum(weights, axis=-1)
        rounded = lax.optimization_barrier(weights.astype(jnp.bfloat16)).astype(jnp.float32)
        summed = summed + jnp.einsum("gqk,kd->gqd", rounded, value_tile.astype(jnp.float32))
        return denom_sum, summed

    start_pair = (jnp.zeros(query_rows.shape[:2], jnp.float32), jnp.zeros(query_rows.shape, jnp.float32))
    denom_sum, summed = lax.fori_loop(0, tiles, second_pass, start_pair)
    return (summed / denom_sum[..., None]).astype(jnp.bfloat16)


def reference(q_arrived, key_value_landed, finish, document_numbers):
    block_list = TRAJECTORY_LEN // ARRIVAL_TOKENS
    q_shaped = q_arrived.reshape(N_REP, block_list, ARRIVAL_TOKENS, QUERY_HEADS * HEAD_SIZE)
    key_value_reshaped = key_value_landed.reshape(N_REP, block_list, ARRIVAL_TOKENS, 2 * KEY_VALUE_HEADS * HEAD_SIZE)
    q_list = []
    key_value_items = []
    for target in range(N_REP):
        q_acc = jnp.zeros((block_list, ARRIVAL_TOKENS, QUERY_HEADS * HEAD_SIZE), jnp.float32)
        key_value_accum = jnp.zeros((block_list, ARRIVAL_TOKENS, 2 * KEY_VALUE_HEADS * HEAD_SIZE), jnp.float32)
        for source in range(N_REP):
            chosen = (finish[:, source] == target)[:, None, None]
            q_acc = q_acc + jnp.where(chosen, q_shaped[source].astype(jnp.float32), 0.0)
            key_value_accum = key_value_accum + jnp.where(chosen, key_value_reshaped[source].astype(jnp.float32), 0.0)
        q_list.append(q_acc.astype(jnp.bfloat16))
        key_value_items.append(key_value_accum.astype(jnp.bfloat16))
    query_trajectory = jnp.stack(q_list).reshape(N_REP, TRAJECTORY_LEN, QUERY_HEADS * HEAD_SIZE)
    key_value_trajectory = jnp.stack(key_value_items).reshape(N_REP, TRAJECTORY_LEN, 2 * KEY_VALUE_HEADS * HEAD_SIZE)
    group_wise = QUERY_HEADS // KEY_VALUE_HEADS
    query_head_list = query_trajectory.reshape(N_REP, TRAJECTORY_LEN, KEY_VALUE_HEADS, group_wise, HEAD_SIZE).transpose(0, 2, 3, 1, 4).reshape(N_REP * KEY_VALUE_HEADS, group_wise, TRAJECTORY_LEN, HEAD_SIZE)
    key_value_head_list = key_value_trajectory.reshape(N_REP, TRAJECTORY_LEN, KEY_VALUE_HEADS, 2, HEAD_SIZE).transpose(0, 2, 3, 1, 4).reshape(N_REP * KEY_VALUE_HEADS, 2, TRAJECTORY_LEN, HEAD_SIZE)
    document_float = jnp.repeat(document_numbers.astype(jnp.float32), KEY_VALUE_HEADS, axis=0)
    positions = jnp.arange(TRAJECTORY_LEN, dtype=jnp.int32)

    def one_head(item):
        query_all, key_value, doc_row = item
        query_blocks = query_all.reshape(group_wise, TRAJECTORY_LEN // TOK_DEV, TOK_DEV, HEAD_SIZE).transpose(1, 0, 2, 3)

        def one_block(piece):
            query_rows, query_pos, query_doc = piece
            return attend(query_rows, key_value[0], key_value[1], query_pos, query_doc, positions, doc_row, 2 * TOK_DEV)

        outcome = lax.map(one_block, (query_blocks, positions.reshape(-1, TOK_DEV), doc_row.reshape(-1, TOK_DEV)))
        return outcome.transpose(1, 0, 2, 3).reshape(group_wise, TRAJECTORY_LEN, HEAD_SIZE)

    attended = lax.map(one_head, (query_head_list, key_value_head_list, document_float))
    return attended.reshape(N_REP, KEY_VALUE_HEADS, group_wise, TRAJECTORY_LEN, HEAD_SIZE).transpose(0, 3, 1, 2, 4).reshape(N_REP, TRAJECTORY_LEN, QUERY_HEADS * HEAD_SIZE)
```

```python
import functools

import jax
import jax.numpy as jnp
from jax import lax
from jax.experimental import pallas as pl
from jax.experimental.pallas import tpu as pltpu
from jax.sharding import PartitionSpec as P

HEAD = 128
BLOCK = 128
UP = 4
DOWN = 3
PIECES = 2
SCALE = HEAD**-0.5 * 1.4426950408889634
HIDE = -float(2**20)
MESH = pl.DeviceIdType.MESH


def kernel(
    reps, ctxs, q_hbm, kv_hbm, fin_hbm, doc_hbm, out_hbm,
    q_in, kv_in, fin, doc, send_kv, send_q, recv_kv, recv_q, kvs, counts, hide, qa, top, acc, out,
    in_sem, x_send, x_recv, cnt_send, cnt_recv, up_send, up_recv, dn_send, dn_recv,
    sib_send, sib_recv, out_sem,
):
    blocks = q_in.shape[0]
    rows = blocks * BLOCK
    heads = q_in.shape[2] // HEAD
    chips = ctxs // 2
    piece = rows // PIECES
    r = lax.axis_index("rep")
    c = lax.axis_index("ctx")
    z = c // 2
    core = c % 2
    above = {"ctx": (c + 2) % ctxs}
    below = {"ctx": (c + ctxs - 2) % ctxs}
    sibling = {"ctx": c + 1 - 2 * core}

    loads = [
        pltpu.make_async_copy(src, dst, in_sem.at[i])
        for i, (src, dst) in enumerate(
            [(fin_hbm, fin), (kv_hbm, kv_in), (q_hbm, q_in), (doc_hbm, doc)]
        )
    ]
    for load in loads:
        load.start()
    barrier = pltpu.get_barrier_semaphore()
    for step in range(1, reps):
        pl.semaphore_signal(barrier, inc=1, device_id={"rep": (r + step) % reps}, device_id_type=MESH)

    def greet(step, _):
        pl.semaphore_signal(barrier, inc=1, device_id={"ctx": (c + step) % ctxs}, device_id_type=MESH)
        return 0

    lax.fori_loop(1, ctxs, greet, 0)

    def block_for(group):
        found = jnp.int32(0)
        for b in range(1, blocks):
            found = jnp.where(fin[b, r] == group, b, found)
        return found

    def source_slot(b):
        source = jnp.int32(0)
        for s in range(1, reps):
            source = jnp.where(fin[b, s] == r, s, source)
        return (r + reps - source) % reps

    def exchange(step, which, src, dst):
        return pltpu.make_async_remote_copy(
            src_ref=src.at[step], dst_ref=dst.at[step],
            send_sem=x_send.at[which, step], recv_sem=x_recv.at[which, step],
            device_id={"rep": (r + step) % reps}, device_id_type=MESH,
        )

    loads[0].wait()
    loads[1].wait()
    targets = [block_for((r + step) % reps) for step in range(reps)]
    for step in range(1, reps):
        send_kv[step] = kv_in[targets[step]]
    pl.semaphore_wait(barrier, reps - 1 + ctxs - 1)
    for step in range(1, reps):
        exchange(step, 0, send_kv, recv_kv).start()
    loads[2].wait()
    for step in range(1, reps):
        send_q[step] = q_in[targets[step]]
        exchange(step, 1, send_q, recv_q).start()
    loads[3].wait()
    doc_row = doc[...]
    lane = lax.broadcasted_iota(jnp.int32, (8, HEAD), 1)
    before = jnp.zeros((8, HEAD), jnp.float32)
    numbers = 4
    for j in range(1, numbers):
        count = jnp.sum((doc_row < j).astype(jnp.float32), axis=1, keepdims=True)
        before = before + jnp.where(lane == j, count, 0.0)
    before = before + jnp.where(lane >= numbers, float(rows), 0.0)
    counts[c] = before

    def count_copy(step):
        return pltpu.make_async_remote_copy(
            src_ref=counts.at[c], dst_ref=counts.at[c],
            send_sem=cnt_send.at[step], recv_sem=cnt_recv.at[step],
            device_id={"ctx": (c + step) % ctxs}, device_id_type=MESH,
        )

    def send_counts(step, _):
        count_copy(step).start()
        return 0

    lax.fori_loop(1, ctxs, send_counts, 0)
    recv_kv[0] = kv_in[targets[0]]
    recv_q[0] = q_in[targets[0]]

    for step in range(1, reps):
        exchange(step, 0, send_kv, recv_kv).wait_recv()
    slots = [source_slot(b) for b in range(blocks)]
    for b in range(blocks):
        kvs[z, pl.ds(pl.multiple_of(core * rows + b * BLOCK, BLOCK), BLOCK), :] = recv_kv[slots[b]]

    def hop(slot, part, k, device, send, recv):
        where = kvs.at[slot, pl.ds(pl.multiple_of(core * rows + part * piece, piece), piece), :]
        return pltpu.make_async_remote_copy(
            src_ref=where, dst_ref=where, send_sem=send.at[k, part], recv_sem=recv.at[k, part],
            device_id=device, device_id_type=MESH,
        )

    def up(slot, part, k):
        return hop(slot, part, k, above, up_send, up_recv)

    def dn(slot, part, k):
        return hop(slot, part, k, below, dn_send, dn_recv)

    def sib(slot, part, k):
        return hop(slot, part, k, sibling, sib_send, sib_recv)

    for part in range(PIECES):
        @pl.when(z < chips - 1)
        def _():
            up(z, part, 1).start()

        @pl.when(z < chips - UP - 1)
        def _():
            dn(z, part, 1).start()

        @pl.when(core == 0)
        def _():
            sib(z, part, 0).start()

    def wait_counts(step, _):
        count_copy(step).wait()
        return 0

    lax.fori_loop(1, ctxs, wait_counts, 0)
    starts = counts[0]
    for i in range(1, ctxs):
        starts = starts + counts[i]
    starts = starts[0:1, :]
    ends = jnp.concatenate([starts[:, 1:], starts[:, HEAD - 1 :]], axis=1)

    def within(first, length):
        at = (lax.broadcasted_iota(jnp.int32, (length, HEAD), 0) + first).astype(jnp.float32)
        return (at >= starts) & (at < ends)

    def fill(slot, _):
        hide[slot] = jnp.where(within(slot * 2 * rows, 2 * rows), 0.0, HIDE).astype(jnp.bfloat16)
        return 0

    lax.fori_loop(0, z + 1, fill, 0)
    own_doc = jnp.where(within(c * rows, rows), 1.0, 0.0).astype(jnp.bfloat16)
    for h in range(heads):
        qa[h * rows : (h + 1) * rows, HEAD:] = own_doc
    for step in range(1, reps):
        exchange(step, 1, send_q, recv_q).wait_recv()
    for b in range(blocks):
        q_block = recv_q[slots[b]]
        for h in range(heads):
            qa[h * rows + b * BLOCK : h * rows + (b + 1) * BLOCK, 0:HEAD] = q_block[:, h * HEAD : (h + 1) * HEAD]

    def unit(slot, first, keys, diagonal):
        span = pl.ds(pl.multiple_of(first, BLOCK), keys)
        key_rows = jnp.concatenate([kvs[slot, span, 0:HEAD], hide[slot, span, :]], axis=1)
        value = kvs[slot, span, HEAD:]
        value_rows = jnp.concatenate([value, jnp.ones_like(value)], axis=1)

        def score(h):
            s = lax.dot_general(
                qa[h * rows : (h + 1) * rows, :], key_rows, (((1,), (1,)), ((), ())),
                preferred_element_type=jnp.float32,
            )
            if diagonal:
                ahead = lax.broadcasted_iota(jnp.int32, s.shape, 1) > lax.broadcasted_iota(jnp.int32, s.shape, 0)
                s = jnp.where(ahead, HIDE, s)
            return s

        def soften(h, s):
            part = slice(h * rows, (h + 1) * rows)
            high = jnp.max(s, axis=1, keepdims=True)
            if diagonal:
                now = jnp.broadcast_to(high, (rows, HEAD))
                decay = None
            else:
                now = jnp.maximum(top[part, :], high)
                decay = jnp.exp2((top[part, :] - now) * SCALE)
            top[part, :] = now
            p = jnp.exp2((s - jnp.concatenate([now] * (keys // HEAD), axis=1)) * SCALE)
            return p.astype(jnp.bfloat16), decay

        def mix(h, p, decay):
            part = slice(h * rows, (h + 1) * rows)
            o = jnp.dot(p, value_rows, preferred_element_type=jnp.float32)
            if diagonal:
                acc[part, :] = o
            else:
                acc[part, :] = acc[part, :] * jnp.concatenate([decay] * 2, axis=1) + o

        scores = {0: score(0)}
        soft = {}
        for h in range(heads + 1):
            if h + 1 < heads:
                scores[h + 1] = score(h + 1)
            if h < heads:
                soft[h] = soften(h, scores.pop(h))
            if h >= 1:
                mix(h - 1, *soft.pop(h - 1))

    unit(z, core * rows, rows, True)

    @pl.when(core == 1)
    def _():
        for part in range(PIECES):
            hop_in(kvs, sib_recv, z, 1 - core, part, 0, rows, piece, sib_send, sibling).wait_recv()
        unit(z, 0, rows, False)

    def receive(k, _):
        slot = (z + chips - k) % chips
        far = (z + k) % chips
        has_up = z >= k
        has_dn = (far < chips - UP - 1) & (k <= DOWN)
        use_dn = has_dn & (z > UP) & (z - far <= chips - 2)
        for part in range(PIECES):
            @pl.when(has_up)
            def _():
                up(slot, part, k).wait_recv()

                @pl.when((k < UP) & (z < chips - 1))
                def _():
                    up(slot, part, k + 1).start()

                sib(slot, part, k).start()

            @pl.when(has_dn)
            def _():
                dn(far, part, k).wait_recv()

                @pl.when(k < DOWN)
                def _():
                    dn(far, part, k + 1).start()

            @pl.when(use_dn)
            def _():
                sib(far, part, UP + k).start()

        @pl.when(has_up)
        def _():
            for part in range(PIECES):
                hop_in(kvs, sib_recv, slot, 1 - core, part, k, rows, piece, sib_send, sibling).wait_recv()
            unit(slot, 0, 2 * rows, False)

        @pl.when(use_dn)
        def _():
            for part in range(PIECES):
                hop_in(kvs, sib_recv, far, 1 - core, part, UP + k, rows, piece, sib_send, sibling).wait_recv()
            unit(far, 0, 2 * rows, False)

        return 0

    lax.fori_loop(1, UP + 1, receive, 0)

    for h in range(heads):
        part = slice(h * rows, (h + 1) * rows)
        out[:, h * HEAD : (h + 1) * HEAD] = (acc[part, 0:HEAD] / acc[part, HEAD:]).astype(jnp.bfloat16)
    result = pltpu.make_async_copy(out, out_hbm.at[0], out_sem)
    result.start()

    for step in range(1, reps):
        exchange(step, 0, send_kv, recv_kv).wait_send()
        exchange(step, 1, send_q, recv_q).wait_send()

    def drain(k, _):
        slot = (z + chips - k) % chips
        far = (z + k) % chips
        has_up = z >= k
        has_dn = (far < chips - UP - 1) & (k <= DOWN)
        use_dn = has_dn & (z > UP) & (z - far <= chips - 2)
        for part in range(PIECES):
            @pl.when(has_up)
            def _():
                @pl.when((k < UP) & (z < chips - 1))
                def _():
                    up(slot, part, k + 1).wait_send()

                sib(slot, part, k).wait_send()

            @pl.when(has_dn & (k < DOWN))
            def _():
                dn(far, part, k + 1).wait_send()

            @pl.when(use_dn)
            def _():
                sib(far, part, UP + k).wait_send()

        return 0

    lax.fori_loop(1, UP + 1, drain, 0)
    for part in range(PIECES):
        @pl.when(z < chips - 1)
        def _():
            up(z, part, 1).wait_send()

        @pl.when(z < chips - UP - 1)
        def _():
            dn(z, part, 1).wait_send()

        @pl.when(core == 0)
        def _():
            sib(z, part, 0).wait_send()

    result.wait()


def hop_in(kvs, recv, slot, core, part, k, rows, piece, send, device):
    where = kvs.at[slot, pl.ds(pl.multiple_of(core * rows + part * piece, piece), piece), :]
    return pltpu.make_async_remote_copy(
        src_ref=where, dst_ref=where, send_sem=send.at[k, part], recv_sem=recv.at[k, part],
        device_id=device, device_id_type=MESH,
    )


def body(q_arrived, key_value_landed, finish, document_numbers):
    rows, q_width = q_arrived.shape[1:]
    kv_width = key_value_landed.shape[2]
    reps = lax.axis_size("rep")
    ctxs = lax.axis_size("ctx")
    chips = ctxs // 2
    heads = q_width // HEAD
    blocks = rows // BLOCK
    bf16, f32 = jnp.bfloat16, jnp.float32
    dma = pltpu.SemaphoreType.DMA
    return pl.pallas_call(
        functools.partial(kernel, reps, ctxs),
        out_shape=jax.ShapeDtypeStruct(q_arrived.shape, bf16),
        in_specs=[pl.BlockSpec(memory_space=pl.ANY)] * 4,
        out_specs=pl.BlockSpec(memory_space=pl.ANY),
        scratch_shapes=[
            pltpu.VMEM((blocks, BLOCK, q_width), bf16),
            pltpu.VMEM((blocks, BLOCK, kv_width), bf16),
            pltpu.SMEM(finish.shape, jnp.int32),
            pltpu.VMEM(document_numbers.shape, jnp.int32),
            pltpu.VMEM((reps, BLOCK, kv_width), bf16),
            pltpu.VMEM((reps, BLOCK, q_width), bf16),
            pltpu.VMEM((reps, BLOCK, kv_width), bf16),
            pltpu.VMEM((reps, BLOCK, q_width), bf16),
            pltpu.VMEM((chips, 2 * rows, kv_width), bf16),
            pltpu.VMEM((ctxs, 8, HEAD), f32),
            pltpu.VMEM((chips, 2 * rows, HEAD), bf16),
            pltpu.VMEM((heads * rows, 2 * HEAD), bf16),
            pltpu.VMEM((heads * rows, HEAD), f32),
            pltpu.VMEM((heads * rows, 2 * HEAD), f32),
            pltpu.VMEM((rows, q_width), bf16),
            dma((4,)),
            dma((2, reps)),
            dma((2, reps)),
            dma((ctxs,)),
            dma((ctxs,)),
            dma((UP + 1, PIECES)),
            dma((UP + 1, PIECES)),
            dma((DOWN + 1, PIECES)),
            dma((DOWN + 1, PIECES)),
            dma((UP + DOWN + 1, PIECES)),
            dma((UP + DOWN + 1, PIECES)),
            dma,
        ],
        compiler_params=pltpu.CompilerParams(
            collective_id=0, has_side_effects=True, vmem_limit_bytes=48 * 2**20
        ),
    )(
        q_arrived.reshape(blocks, BLOCK, q_width),
        key_value_landed.reshape(blocks, BLOCK, kv_width),
        finish,
        document_numbers,
    )


def solution(mesh):
    in_specs = (P("rep", "ctx", "tp"), P("rep", "ctx", "tp"), P("ctx", None), P("rep", "ctx"))
    out_specs = P("rep", "ctx", "tp")
    return jax.shard_map(body, mesh=mesh, in_specs=in_specs, out_specs=out_specs, check_vma=False)
```

```python
import functools

import jax
import jax.numpy as jnp
from jax import lax
from jax.experimental import pallas as pl
from jax.experimental.pallas import tpu as pltpu
from jax.sharding import PartitionSpec as P

HEAD = 128
BLOCK = 128
NOTE = 16
NUMBERS = 4
UP = 4
PARTS = 2
SCALE = HEAD**-0.5 * 1.4426950408889634
HIDE = -float(2**20)
MESH = pl.DeviceIdType.MESH


def kernel(
    reps, ctxs, q_hbm, kv_hbm, fin_hbm, doc_hbm, out_hbm,
    q_in, kv_in, fin, doc, send_kv, send_q, recv_kv, recv_q, kvs, qa, top, acc, out,
    in_sem, x_send, x_recv, ready, up_send, up_recv, far_send, far_recv, sib_send, sib_recv, out_sem,
):
    blocks = q_in.shape[0]
    rows = blocks * BLOCK
    span = rows + NOTE
    heads = q_in.shape[2] // HEAD
    chips = ctxs // 2
    last = chips - 1
    half_rows = rows // PARTS
    pieces = [(p * half_rows, half_rows + (NOTE if p == PARTS - 1 else 0)) for p in range(PARTS)]
    r = lax.axis_index("rep")
    c = lax.axis_index("ctx")
    z = c // 2
    core = c % 2

    def on_chip(chip):
        return {"ctx": chip * 2 + core}

    above = on_chip((z + 1) % chips)
    below = on_chip((z + last) % chips)
    sibling = {"ctx": c + 1 - 2 * core}

    def signal(sem, device):
        pl.semaphore_signal(sem, inc=1, device_id=device, device_id_type=MESH)

    loads = [
        pltpu.make_async_copy(src, dst, in_sem.at[i])
        for i, (src, dst) in enumerate([(fin_hbm, fin), (kv_hbm, kv_in), (q_hbm, q_in), (doc_hbm, doc)])
    ]
    for load in loads:
        load.start()
    barrier = pltpu.get_barrier_semaphore()
    for step in range(1, reps):
        signal(barrier, {"rep": (r + step) % reps})
    signal(barrier, sibling)

    @pl.when(z < last)
    def _():
        signal(barrier, above)

    @pl.when(z == 0)
    def _():
        for chip in (2, last - 1, last):
            signal(barrier, on_chip(chip))

    def block_for(group):
        found = jnp.int32(0)
        for b in range(1, blocks):
            found = jnp.where(fin[b, r] == group, b, found)
        return found

    def source_slot(b):
        source = jnp.int32(0)
        for s in range(1, reps):
            source = jnp.where(fin[b, s] == r, s, source)
        return (r + reps - source) % reps

    def exchange(step, which, src, dst):
        return pltpu.make_async_remote_copy(
            src_ref=src.at[step], dst_ref=dst.at[step],
            send_sem=x_send.at[which, step], recv_sem=x_recv.at[which, step],
            device_id={"rep": (r + step) % reps}, device_id_type=MESH,
        )

    loads[0].wait()
    loads[1].wait()
    targets = [block_for((r + step) % reps) for step in range(reps)]
    for step in range(1, reps):
        send_kv[step] = kv_in[targets[step]]
    pl.semaphore_wait(
        barrier,
        reps + jnp.where(z > 0, 1, 0) + jnp.where((z == 2) | (z >= last - 1), 1, 0),
    )
    @pl.when(z > 0)
    def _():
        signal(ready.at[0], below)

    @pl.when(z == last - 1)
    def _():
        signal(ready.at[1], on_chip(0))

    @pl.when(z == last)
    def _():
        signal(ready.at[2], on_chip(0))

    for step in range(1, reps):
        exchange(step, 0, send_kv, recv_kv).start()
    loads[2].wait()
    for step in range(1, reps):
        send_q[step] = q_in[targets[step]]
        exchange(step, 1, send_q, recv_q).start()
    loads[3].wait()
    doc_row = doc[...]
    lane = lax.broadcasted_iota(jnp.int32, (NOTE, HEAD), 1)
    starts = jnp.where(lane >= NUMBERS, float(rows), 0.0)
    ends = jnp.where(lane >= NUMBERS - 1, float(rows), 0.0)
    for j in range(1, NUMBERS):
        count = jnp.sum((doc_row < j).astype(jnp.float32), axis=1, keepdims=True)
        starts = starts + jnp.where(lane == j, count, 0.0)
        ends = ends + jnp.where(lane == j - 1, count, 0.0)

    def in_two(count):
        most = float(rows // 2)
        line = lax.broadcasted_iota(jnp.int32, (NOTE, HEAD), 0)
        low = jnp.minimum(count, most)
        return jnp.where(line == 0, low, jnp.where(line == 1, count - low, 0.0)).astype(jnp.bfloat16)

    def place(half, first, length):
        return pl.ds(pl.multiple_of(half * span + first, 16), length)

    kvs[z, place(core, rows, NOTE), 0:HEAD] = in_two(starts)
    kvs[z, place(core, rows, NOTE), HEAD:] = in_two(ends)

    def within(starts, ends):
        at = lax.broadcasted_iota(jnp.int32, (rows, HEAD), 0).astype(jnp.float32)
        return (at >= starts) & (at < ends)

    own_doc = jnp.where(within(starts[0:1, :], ends[0:1, :]), 1.0, 0.0).astype(jnp.bfloat16)
    for h in range(heads):
        qa[h * rows : (h + 1) * rows, HEAD:] = own_doc
    recv_kv[0] = kv_in[targets[0]]
    recv_q[0] = q_in[targets[0]]

    for step in range(1, reps):
        exchange(step, 0, send_kv, recv_kv).wait_recv()
    slots = [source_slot(b) for b in range(blocks)]
    for b in range(blocks):
        kvs[z, place(core, b * BLOCK, BLOCK), :] = recv_kv[slots[b]]

    def hop(slot, half, part, device, send, recv, k):
        where = kvs.at[slot, place(half, *pieces[part]), :]
        return pltpu.make_async_remote_copy(
            src_ref=where, dst_ref=where, send_sem=send.at[k, part], recv_sem=recv.at[k, part],
            device_id=device, device_id_type=MESH,
        )

    def up(slot, part, k):
        return hop(slot, core, part, above, up_send, up_recv, k)

    def far(slot, part, device):
        return hop(slot, core, part, device, far_send, far_recv, slot)

    def sib(slot, part, k):
        return hop(slot, core, part, sibling, sib_send, sib_recv, k)

    def from_sib(slot, k):
        for part in range(PARTS):
            hop(slot, 1 - core, part, sibling, sib_send, sib_recv, k).wait_recv()

    @pl.when(z < last)
    def _():
        pl.semaphore_wait(ready.at[0], 1)
        for part in range(PARTS):
            up(z, part, 1).start()

    @pl.when((z == 1) | (z == 2))
    def _():
        for part in range(PARTS):
            far(z, part, on_chip(0)).start()

    @pl.when(core == 0)
    def _():
        for part in range(PARTS):
            sib(z, part, 0).start()

    def has_far(k):
        return ((k == 2) & (z >= last - 1)) | ((k == 3) & ((z == last) | (z == last - 2))) | ((k == 4) & (z == last - 1))

    def far_number(k):
        return jnp.where(k == 2, 1, 2)

    def far_slot(k):
        return jnp.maximum(z - last + far_number(k), 0)

    def take_up(k):
        slot = (z + chips - k) % chips

        @pl.when(z >= k)
        def _():
            for part in range(PARTS):
                up(slot, part, k).wait_recv()

                @pl.when((k < UP) & (z < last))
                def _():
                    up(slot, part, k + 1).start()

                sib(slot, part, k).start()

    def take_far(k):
        for part in range(PARTS):
            far(far_slot(k), part, below).wait_recv()

            @pl.when(k == 2)
            def _():
                far(far_slot(k), part, below).start()

            sib(far_slot(k), part, UP + far_number(k)).start()

    take_up(1)

    @pl.when(z == last - 1)
    def _():
        take_far(2)

    for step in range(1, reps):
        exchange(step, 1, send_q, recv_q).wait_recv()
    for b in range(blocks):
        q_block = recv_q[slots[b]]
        for h in range(heads):
            qa[h * rows + b * BLOCK : h * rows + (b + 1) * BLOCK, 0:HEAD] = q_block[:, h * HEAD : (h + 1) * HEAD]

    def unit(slot, halves, diagonal):
        key_rows, value_rows = [], []
        for half in halves:
            note = kvs[slot, place(half, rows, NOTE), :].astype(jnp.float32)
            note = note[0:1, :] + note[1:2, :]
            hide = jnp.where(within(note[:, 0:HEAD], note[:, HEAD:]), 0.0, HIDE).astype(jnp.bfloat16)
            keys = kvs[slot, place(half, 0, rows), 0:HEAD]
            values = kvs[slot, place(half, 0, rows), HEAD:]
            key_rows.append(jnp.concatenate([keys, hide], axis=1))
            value_rows.append(jnp.concatenate([values, jnp.ones_like(values)], axis=1))
        key_rows = jnp.concatenate(key_rows, axis=0)
        value_rows = jnp.concatenate(value_rows, axis=0)

        def score(h):
            s = lax.dot_general(
                qa[h * rows : (h + 1) * rows, :], key_rows, (((1,), (1,)), ((), ())),
                preferred_element_type=jnp.float32,
            )
            if diagonal:
                ahead = lax.broadcasted_iota(jnp.int32, s.shape, 1) > lax.broadcasted_iota(jnp.int32, s.shape, 0)
                s = jnp.where(ahead, HIDE, s)
            return s

        def soften(h, s):
            part = slice(h * rows, (h + 1) * rows)
            high = jnp.max(s, axis=1, keepdims=True)
            if diagonal:
                now = jnp.broadcast_to(high, (rows, HEAD))
                decay = None
            else:
                now = jnp.maximum(top[part, :], high)
                decay = jnp.exp2((top[part, :] - now) * SCALE)
            top[part, :] = now
            p = jnp.exp2((s - jnp.concatenate([now] * (s.shape[1] // HEAD), axis=1)) * SCALE)
            return p.astype(jnp.bfloat16), decay

        def mix(h, p, decay):
            part = slice(h * rows, (h + 1) * rows)
            o = jnp.dot(p, value_rows, preferred_element_type=jnp.float32)
            if diagonal:
                acc[part, :] = o
            else:
                acc[part, :] = acc[part, :] * jnp.concatenate([decay] * 2, axis=1) + o

        scores = {0: score(0)}
        soft = {}
        for h in range(heads + 1):
            if h + 1 < heads:
                scores[h + 1] = score(h + 1)
            if h < heads:
                soft[h] = soften(h, scores.pop(h))
            if h >= 1:
                mix(h - 1, *soft.pop(h - 1))

    unit(z, [core], True)

    @pl.when(z == 0)
    def _():
        pl.semaphore_wait(ready.at[1], 1)
        for part in range(PARTS):
            far(0, part, on_chip(last - 1)).start()
        pl.semaphore_wait(ready.at[2], 1)
        for slot in (1, 2):
            for part in range(PARTS):
                far(slot, part, on_chip(last)).wait_recv()
                far(slot, part, on_chip(last)).start()

    @pl.when(core == 1)
    def _():
        from_sib(z, 0)
        unit(z, [0], False)

    def receive(k, _):
        @pl.when(z >= k)
        def _():
            slot = (z + chips - k) % chips
            from_sib(slot, k)
            unit(slot, [0, 1], False)

        @pl.when(k < UP)
        def _():
            take_up(k + 1)

        @pl.when((k == 1) & (z == last))
        def _():
            take_far(2)

        @pl.when(has_far(k))
        def _():
            @pl.when(k > 2)
            def _():
                take_far(k)

            from_sib(far_slot(k), UP + far_number(k))
            unit(far_slot(k), [0, 1], False)

        return 0

    lax.fori_loop(1, UP + 1, receive, 0)

    for h in range(heads):
        part = slice(h * rows, (h + 1) * rows)
        out[:, h * HEAD : (h + 1) * HEAD] = (acc[part, 0:HEAD] / acc[part, HEAD:]).astype(jnp.bfloat16)
    result = pltpu.make_async_copy(out, out_hbm.at[0], out_sem)
    result.start()

    for step in range(1, reps):
        exchange(step, 0, send_kv, recv_kv).wait_send()
        exchange(step, 1, send_q, recv_q).wait_send()

    def drain(k, _):
        slot = (z + chips - k) % chips
        for part in range(PARTS):
            @pl.when(z >= k)
            def _():
                @pl.when((k < UP) & (z < last))
                def _():
                    up(slot, part, k + 1).wait_send()

                sib(slot, part, k).wait_send()

            @pl.when(has_far(k))
            def _():
                @pl.when(k == 2)
                def _():
                    far(far_slot(k), part, below).wait_send()

                sib(far_slot(k), part, UP + far_number(k)).wait_send()

        return 0

    lax.fori_loop(1, UP + 1, drain, 0)
    for part in range(PARTS):
        @pl.when(z < last)
        def _():
            up(z, part, 1).wait_send()

        @pl.when((z == 1) | (z == 2))
        def _():
            far(z, part, on_chip(0)).wait_send()

        @pl.when(z == 0)
        def _():
            for slot in range(3):
                far(slot, part, on_chip(last)).wait_send()

        @pl.when(core == 0)
        def _():
            sib(z, part, 0).wait_send()

    result.wait()


def body(q_arrived, key_value_landed, finish, document_numbers):
    rows, q_width = q_arrived.shape[1:]
    kv_width = key_value_landed.shape[2]
    reps = lax.axis_size("rep")
    ctxs = lax.axis_size("ctx")
    heads = q_width // HEAD
    blocks = rows // BLOCK
    bf16, f32 = jnp.bfloat16, jnp.float32
    dma = pltpu.SemaphoreType.DMA
    return pl.pallas_call(
        functools.partial(kernel, reps, ctxs),
        out_shape=jax.ShapeDtypeStruct(q_arrived.shape, bf16),
        in_specs=[pl.BlockSpec(memory_space=pl.ANY)] * 4,
        out_specs=pl.BlockSpec(memory_space=pl.ANY),
        scratch_shapes=[
            pltpu.VMEM((blocks, BLOCK, q_width), bf16),
            pltpu.VMEM((blocks, BLOCK, kv_width), bf16),
            pltpu.SMEM(finish.shape, jnp.int32),
            pltpu.VMEM(document_numbers.shape, jnp.int32),
            pltpu.VMEM((reps, BLOCK, kv_width), bf16),
            pltpu.VMEM((reps, BLOCK, q_width), bf16),
            pltpu.VMEM((reps, BLOCK, kv_width), bf16),
            pltpu.VMEM((reps, BLOCK, q_width), bf16),
            pltpu.VMEM((ctxs // 2, 2 * (rows + NOTE), kv_width), bf16),
            pltpu.VMEM((heads * rows, 2 * HEAD), bf16),
            pltpu.VMEM((heads * rows, HEAD), f32),
            pltpu.VMEM((heads * rows, 2 * HEAD), f32),
            pltpu.VMEM((rows, q_width), bf16),
            dma((4,)),
            dma((2, reps)),
            dma((2, reps)),
            pltpu.SemaphoreType.REGULAR((3,)),
            dma((UP + 1, PARTS)),
            dma((UP + 1, PARTS)),
            dma((3, PARTS)),
            dma((3, PARTS)),
            dma((UP + 3, PARTS)),
            dma((UP + 3, PARTS)),
            dma,
        ],
        compiler_params=pltpu.CompilerParams(
            collective_id=0, has_side_effects=True, vmem_limit_bytes=62 * 2**20
        ),
    )(
        q_arrived.reshape(blocks, BLOCK, q_width),
        key_value_landed.reshape(blocks, BLOCK, kv_width),
        finish,
        document_numbers,
    )


def solution(mesh):
    in_specs = (P("rep", "ctx", "tp"), P("rep", "ctx", "tp"), P("ctx", None), P("rep", "ctx"))
    out_specs = P("rep", "ctx", "tp")
    return jax.shard_map(body, mesh=mesh, in_specs=in_specs, out_specs=out_specs, check_vma=False)
```

```python
import functools

import jax
import jax.numpy as jnp
from jax import lax
from jax.experimental import pallas as pl
from jax.experimental.pallas import tpu as pltpu
from jax.sharding import PartitionSpec as P

HEAD = 128
BLOCK = 128
NOTE = 16
NUMBERS = 4
UP = 4
PARTS = 2
SCALE = HEAD**-0.5 * 1.4426950408889634
HIDE = -float(2**20)
MESH = pl.DeviceIdType.MESH


def kernel(
    reps, ctxs, q_hbm, kv_hbm, fin_hbm, doc_hbm, out_hbm,
    q_in, kv_in, fin, doc, send_kv, send_q, recv_kv, recv_q, kvs, qa, top, acc, out,
    in_sem, x_send, x_recv, ready, up_send, up_recv, far_send, far_recv, sib_send, sib_recv, out_sem,
):
    blocks = q_in.shape[0]
    rows = blocks * BLOCK
    span = rows + NOTE
    heads = q_in.shape[2] // HEAD
    chips = ctxs // 2
    last = chips - 1
    half_rows = rows // PARTS
    pieces = [(p * half_rows, half_rows + (NOTE if p == PARTS - 1 else 0)) for p in range(PARTS)]
    r = lax.axis_index("rep")
    c = lax.axis_index("ctx")
    z = c // 2
    core = c % 2

    def on_chip(chip):
        return {"ctx": chip * 2 + core}

    above = on_chip((z + 1) % chips)
    below = on_chip((z + last) % chips)
    sibling = {"ctx": c + 1 - 2 * core}

    def signal(sem, device):
        pl.semaphore_signal(sem, inc=1, device_id=device, device_id_type=MESH)

    loads = [
        pltpu.make_async_copy(src, dst, in_sem.at[i])
        for i, (src, dst) in enumerate([(fin_hbm, fin), (kv_hbm, kv_in), (q_hbm, q_in), (doc_hbm, doc)])
    ]
    for load in loads:
        load.start()
    barrier = pltpu.get_barrier_semaphore()
    for step in range(1, reps):
        signal(barrier, {"rep": (r + step) % reps})
    signal(barrier, sibling)

    @pl.when(z < last)
    def _():
        signal(barrier, above)

    @pl.when(z == 0)
    def _():
        for chip in (2, last - 1, last):
            signal(barrier, on_chip(chip))

    def block_for(group):
        found = jnp.int32(0)
        for b in range(1, blocks):
            found = jnp.where(fin[b, r] == group, b, found)
        return found

    def source_slot(b):
        source = jnp.int32(0)
        for s in range(1, reps):
            source = jnp.where(fin[b, s] == r, s, source)
        return (r + reps - source) % reps

    def exchange(step, which, src, dst):
        return pltpu.make_async_remote_copy(
            src_ref=src.at[step], dst_ref=dst.at[step],
            send_sem=x_send.at[which, step], recv_sem=x_recv.at[which, step],
            device_id={"rep": (r + step) % reps}, device_id_type=MESH,
        )

    loads[0].wait()
    loads[1].wait()
    targets = [block_for((r + step) % reps) for step in range(reps)]
    for step in range(1, reps):
        send_kv[step] = kv_in[targets[step]]
    pl.semaphore_wait(
        barrier,
        reps + jnp.where(z > 0, 1, 0) + jnp.where((z == 2) | (z >= last - 1), 1, 0),
    )
    @pl.when(z > 0)
    def _():
        signal(ready.at[0], below)

    @pl.when(z == last - 1)
    def _():
        signal(ready.at[1], on_chip(0))

    @pl.when(z == last)
    def _():
        signal(ready.at[2], on_chip(0))

    for step in range(1, reps):
        exchange(step, 0, send_kv, recv_kv).start()
    loads[2].wait()
    for step in range(1, reps):
        send_q[step] = q_in[targets[step]]
        exchange(step, 1, send_q, recv_q).start()
    loads[3].wait()
    doc_row = doc[...]
    lane = lax.broadcasted_iota(jnp.int32, (NOTE, HEAD), 1)
    starts = jnp.where(lane >= NUMBERS, float(rows), 0.0)
    ends = jnp.where(lane >= NUMBERS - 1, float(rows), 0.0)
    for j in range(1, NUMBERS):
        count = jnp.sum((doc_row < j).astype(jnp.float32), axis=1, keepdims=True)
        starts = starts + jnp.where(lane == j, count, 0.0)
        ends = ends + jnp.where(lane == j - 1, count, 0.0)

    def in_two(count):
        most = float(rows // 2)
        line = lax.broadcasted_iota(jnp.int32, (NOTE, HEAD), 0)
        low = jnp.minimum(count, most)
        return jnp.where(line == 0, low, jnp.where(line == 1, count - low, 0.0)).astype(jnp.bfloat16)

    def place(half, first, length):
        return pl.ds(pl.multiple_of(half * span + first, 16), length)

    kvs[z, place(core, rows, NOTE), 0:HEAD] = in_two(starts)
    kvs[z, place(core, rows, NOTE), HEAD:] = in_two(ends)

    def within(starts, ends):
        at = lax.broadcasted_iota(jnp.int32, (rows, HEAD), 0).astype(jnp.float32)
        return (at >= starts) & (at < ends)

    own_doc = jnp.where(within(starts[0:1, :], ends[0:1, :]), 1.0, 0.0).astype(jnp.bfloat16)
    for h in range(heads):
        qa[h * rows : (h + 1) * rows, HEAD:] = own_doc
    recv_kv[0] = kv_in[targets[0]]
    recv_q[0] = q_in[targets[0]]

    for step in range(1, reps):
        exchange(step, 0, send_kv, recv_kv).wait_recv()
    slots = [source_slot(b) for b in range(blocks)]
    for b in range(blocks):
        kvs[z, place(core, b * BLOCK, BLOCK), :] = recv_kv[slots[b]]

    def hop(slot, half, part, device, send, recv, k):
        where = kvs.at[slot, place(half, *pieces[part]), :]
        return pltpu.make_async_remote_copy(
            src_ref=where, dst_ref=where, send_sem=send.at[k, part], recv_sem=recv.at[k, part],
            device_id=device, device_id_type=MESH,
        )

    def up(slot, part, k):
        return hop(slot, core, part, above, up_send, up_recv, k)

    def far(slot, part, device):
        return hop(slot, core, part, device, far_send, far_recv, slot)

    def sib(slot, part, k):
        return hop(slot, core, part, sibling, sib_send, sib_recv, k)

    def from_sib(slot, k):
        for part in range(PARTS):
            hop(slot, 1 - core, part, sibling, sib_send, sib_recv, k).wait_recv()

    @pl.when(z < last)
    def _():
        pl.semaphore_wait(ready.at[0], 1)
        for part in range(PARTS):
            up(z, part, 1).start()

    @pl.when((z == 1) | (z == 2))
    def _():
        for part in range(PARTS):
            far(z, part, on_chip(0)).start()

    @pl.when(core == 0)
    def _():
        for part in range(PARTS):
            sib(z, part, 0).start()

    def has_far(k):
        first = (k == 2) & (z >= last - 1)
        second = ((k == 3) & (z == last)) | ((k == 4) & ((z == last - 1) | (z == last - 2)))
        return first | second

    def far_number(k):
        return jnp.where(k == 2, 1, 2)

    def far_slot(k):
        return jnp.maximum(z - last + far_number(k), 0)

    def take_up(k):
        slot = (z + chips - k) % chips

        @pl.when(z >= k)
        def _():
            for part in range(PARTS):
                up(slot, part, k).wait_recv()

                @pl.when((k < UP) & (z < last))
                def _():
                    up(slot, part, k + 1).start()

                sib(slot, part, k).start()

    def take_far(k):
        for part in range(PARTS):
            far(far_slot(k), part, below).wait_recv()

            @pl.when(k == 2)
            def _():
                far(far_slot(k), part, below).start()

            sib(far_slot(k), part, UP + far_number(k)).start()

    take_up(1)

    @pl.when(z == 0)
    def _():
        pl.semaphore_wait(ready.at[1], 1)
        for part in range(PARTS):
            far(0, part, on_chip(last - 1)).start()
        pl.semaphore_wait(ready.at[2], 1)
        for slot in (1, 2):
            for part in range(PARTS):
                far(slot, part, on_chip(last)).wait_recv()
                far(slot, part, on_chip(last)).start()

    for step in range(1, reps):
        exchange(step, 1, send_q, recv_q).wait_recv()
    for b in range(blocks):
        q_block = recv_q[slots[b]]
        for h in range(heads):
            qa[h * rows + b * BLOCK : h * rows + (b + 1) * BLOCK, 0:HEAD] = q_block[:, h * HEAD : (h + 1) * HEAD]

    def unit(slot, halves, diagonal):
        key_rows, value_rows = [], []
        for half in halves:
            note = kvs[slot, place(half, rows, NOTE), :].astype(jnp.float32)
            note = note[0:1, :] + note[1:2, :]
            hide = jnp.where(within(note[:, 0:HEAD], note[:, HEAD:]), 0.0, HIDE).astype(jnp.bfloat16)
            keys = kvs[slot, place(half, 0, rows), 0:HEAD]
            values = kvs[slot, place(half, 0, rows), HEAD:]
            key_rows.append(jnp.concatenate([keys, hide], axis=1))
            value_rows.append(jnp.concatenate([values, jnp.ones_like(values)], axis=1))
        key_rows = jnp.concatenate(key_rows, axis=0)
        value_rows = jnp.concatenate(value_rows, axis=0)

        def score(h):
            s = lax.dot_general(
                qa[h * rows : (h + 1) * rows, :], key_rows, (((1,), (1,)), ((), ())),
                preferred_element_type=jnp.float32,
            )
            if diagonal:
                ahead = lax.broadcasted_iota(jnp.int32, s.shape, 1) > lax.broadcasted_iota(jnp.int32, s.shape, 0)
                s = jnp.where(ahead, HIDE, s)
            return s

        def soften(h, s):
            part = slice(h * rows, (h + 1) * rows)
            high = jnp.max(s, axis=1, keepdims=True)
            if diagonal:
                now = jnp.broadcast_to(high, (rows, HEAD))
                decay = None
            else:
                now = jnp.maximum(top[part, :], high)
                decay = jnp.exp2((top[part, :] - now) * SCALE)
            top[part, :] = now
            p = jnp.exp2((s - jnp.concatenate([now] * (s.shape[1] // HEAD), axis=1)) * SCALE)
            return p.astype(jnp.bfloat16), decay

        def mix(h, p, decay):
            part = slice(h * rows, (h + 1) * rows)
            o = jnp.dot(p, value_rows, preferred_element_type=jnp.float32)
            if diagonal:
                acc[part, :] = o
            else:
                acc[part, :] = acc[part, :] * jnp.concatenate([decay] * 2, axis=1) + o

        scores = {0: score(0)}
        soft = {}
        for h in range(heads + 1):
            if h + 1 < heads:
                scores[h + 1] = score(h + 1)
            if h < heads:
                soft[h] = soften(h, scores.pop(h))
            if h >= 1:
                mix(h - 1, *soft.pop(h - 1))

    unit(z, [core], True)

    @pl.when(core == 1)
    def _():
        from_sib(z, 0)
        unit(z, [0], False)

    def receive(k, _):
        @pl.when(has_far(k))
        def _():
            take_far(k)

        @pl.when(z >= k)
        def _():
            slot = (z + chips - k) % chips
            from_sib(slot, k)
            unit(slot, [0, 1], False)

        @pl.when(has_far(k))
        def _():
            from_sib(far_slot(k), UP + far_number(k))
            unit(far_slot(k), [0, 1], False)

        @pl.when(k < UP)
        def _():
            take_up(k + 1)

        return 0

    lax.fori_loop(1, UP + 1, receive, 0)

    for h in range(heads):
        part = slice(h * rows, (h + 1) * rows)
        out[:, h * HEAD : (h + 1) * HEAD] = (acc[part, 0:HEAD] / acc[part, HEAD:]).astype(jnp.bfloat16)
    result = pltpu.make_async_copy(out, out_hbm.at[0], out_sem)
    result.start()

    for step in range(1, reps):
        exchange(step, 0, send_kv, recv_kv).wait_send()
        exchange(step, 1, send_q, recv_q).wait_send()

    def drain(k, _):
        slot = (z + chips - k) % chips
        for part in range(PARTS):
            @pl.when(z >= k)
            def _():
                @pl.when((k < UP) & (z < last))
                def _():
                    up(slot, part, k + 1).wait_send()

                sib(slot, part, k).wait_send()

            @pl.when(has_far(k))
            def _():
                @pl.when(k == 2)
                def _():
                    far(far_slot(k), part, below).wait_send()

                sib(far_slot(k), part, UP + far_number(k)).wait_send()

        return 0

    lax.fori_loop(1, UP + 1, drain, 0)
    for part in range(PARTS):
        @pl.when(z < last)
        def _():
            up(z, part, 1).wait_send()

        @pl.when((z == 1) | (z == 2))
        def _():
            far(z, part, on_chip(0)).wait_send()

        @pl.when(z == 0)
        def _():
            for slot in range(3):
                far(slot, part, on_chip(last)).wait_send()

        @pl.when(core == 0)
        def _():
            sib(z, part, 0).wait_send()

    result.wait()


def body(q_arrived, key_value_landed, finish, document_numbers):
    rows, q_width = q_arrived.shape[1:]
    kv_width = key_value_landed.shape[2]
    reps = lax.axis_size("rep")
    ctxs = lax.axis_size("ctx")
    heads = q_width // HEAD
    blocks = rows // BLOCK
    bf16, f32 = jnp.bfloat16, jnp.float32
    dma = pltpu.SemaphoreType.DMA
    return pl.pallas_call(
        functools.partial(kernel, reps, ctxs),
        out_shape=jax.ShapeDtypeStruct(q_arrived.shape, bf16),
        in_specs=[pl.BlockSpec(memory_space=pl.ANY)] * 4,
        out_specs=pl.BlockSpec(memory_space=pl.ANY),
        scratch_shapes=[
            pltpu.VMEM((blocks, BLOCK, q_width), bf16),
            pltpu.VMEM((blocks, BLOCK, kv_width), bf16),
            pltpu.SMEM(finish.shape, jnp.int32),
            pltpu.VMEM(document_numbers.shape, jnp.int32),
            pltpu.VMEM((reps, BLOCK, kv_width), bf16),
            pltpu.VMEM((reps, BLOCK, q_width), bf16),
            pltpu.VMEM((reps, BLOCK, kv_width), bf16),
            pltpu.VMEM((reps, BLOCK, q_width), bf16),
            pltpu.VMEM((ctxs // 2, 2 * (rows + NOTE), kv_width), bf16),
            pltpu.VMEM((heads * rows, 2 * HEAD), bf16),
            pltpu.VMEM((heads * rows, HEAD), f32),
            pltpu.VMEM((heads * rows, 2 * HEAD), f32),
            pltpu.VMEM((rows, q_width), bf16),
            dma((4,)),
            dma((2, reps)),
            dma((2, reps)),
            pltpu.SemaphoreType.REGULAR((3,)),
            dma((UP + 1, PARTS)),
            dma((UP + 1, PARTS)),
            dma((3, PARTS)),
            dma((3, PARTS)),
            dma((UP + 3, PARTS)),
            dma((UP + 3, PARTS)),
            dma,
        ],
        compiler_params=pltpu.CompilerParams(
            collective_id=0, has_side_effects=True, vmem_limit_bytes=62 * 2**20
        ),
    )(
        q_arrived.reshape(blocks, BLOCK, q_width),
        key_value_landed.reshape(blocks, BLOCK, kv_width),
        finish,
        document_numbers,
    )


def solution(mesh):
    in_specs = (P("rep", "ctx", "tp"), P("rep", "ctx", "tp"), P("ctx", None), P("rep", "ctx"))
    out_specs = P("rep", "ctx", "tp")
    return jax.shard_map(body, mesh=mesh, in_specs=in_specs, out_specs=out_specs, check_vma=False)
```

```python
import functools

import jax
import jax.numpy as jnp
from jax import lax
from jax.experimental import pallas as pl
from jax.experimental.pallas import tpu as pltpu
from jax.sharding import PartitionSpec as P

HEAD = 128
BLOCK = 128
NOTE = 16
NUMBERS = 4
UP = 4
PARTS = 2
SCALE = HEAD**-0.5 * 1.4426950408889634
HIDE = -float(2**20)
MESH = pl.DeviceIdType.MESH


def kernel(
    reps, ctxs, q_hbm, kv_hbm, fin_hbm, doc_hbm, out_hbm,
    q_in, kv_in, fin, doc, send_kv, send_q, recv_kv, recv_q, kvs, qa, top, acc, out,
    in_sem, x_send, x_recv, ready, up_send, up_recv, far_send, far_recv, sib_send, sib_recv, out_sem,
):
    blocks = q_in.shape[0]
    rows = blocks * BLOCK
    span = rows + NOTE
    heads = q_in.shape[2] // HEAD
    chips = ctxs // 2
    last = chips - 1
    half_rows = rows // PARTS
    pieces = [(p * half_rows, half_rows + (NOTE if p == PARTS - 1 else 0)) for p in range(PARTS)]
    r = lax.axis_index("rep")
    c = lax.axis_index("ctx")
    z = c // 2
    core = c % 2

    def on_chip(chip):
        return {"ctx": chip * 2 + core}

    above = on_chip((z + 1) % chips)
    below = on_chip((z + last) % chips)
    sibling = {"ctx": c + 1 - 2 * core}

    def signal(sem, device):
        pl.semaphore_signal(sem, inc=1, device_id=device, device_id_type=MESH)

    loads = [
        pltpu.make_async_copy(src, dst, in_sem.at[i])
        for i, (src, dst) in enumerate([(fin_hbm, fin), (kv_hbm, kv_in), (q_hbm, q_in), (doc_hbm, doc)])
    ]
    for load in loads:
        load.start()
    barrier = pltpu.get_barrier_semaphore()
    for step in range(1, reps):
        signal(barrier, {"rep": (r + step) % reps})
    signal(barrier, sibling)

    @pl.when(z < last)
    def _():
        signal(barrier, above)

    @pl.when(z == 0)
    def _():
        for chip in (2, last - 1, last):
            signal(barrier, on_chip(chip))

    def block_for(group):
        found = jnp.int32(0)
        for b in range(1, blocks):
            found = jnp.where(fin[b, r] == group, b, found)
        return found

    def source_slot(b):
        source = jnp.int32(0)
        for s in range(1, reps):
            source = jnp.where(fin[b, s] == r, s, source)
        return (r + reps - source) % reps

    def exchange(step, which, src, dst):
        return pltpu.make_async_remote_copy(
            src_ref=src.at[step], dst_ref=dst.at[step],
            send_sem=x_send.at[which, step], recv_sem=x_recv.at[which, step],
            device_id={"rep": (r + step) % reps}, device_id_type=MESH,
        )

    loads[0].wait()
    loads[1].wait()
    targets = [block_for((r + step) % reps) for step in range(reps)]
    for step in range(1, reps):
        send_kv[step] = kv_in[targets[step]]
    pl.semaphore_wait(
        barrier,
        reps + jnp.where(z > 0, 1, 0) + jnp.where((z == 2) | (z >= last - 1), 1, 0),
    )
    @pl.when(z > 0)
    def _():
        signal(ready.at[0], below)

    @pl.when(z == last - 1)
    def _():
        signal(ready.at[1], on_chip(0))

    @pl.when(z == last)
    def _():
        signal(ready.at[2], on_chip(0))

    for step in range(1, reps):
        exchange(step, 0, send_kv, recv_kv).start()
    loads[2].wait()
    for step in range(1, reps):
        send_q[step] = q_in[targets[step]]
        exchange(step, 1, send_q, recv_q).start()
    loads[3].wait()
    doc_row = doc[...]
    lane = lax.broadcasted_iota(jnp.int32, (NOTE, HEAD), 1)
    starts = jnp.where(lane >= NUMBERS, float(rows), 0.0)
    ends = jnp.where(lane >= NUMBERS - 1, float(rows), 0.0)
    for j in range(1, NUMBERS):
        count = jnp.sum((doc_row < j).astype(jnp.float32), axis=1, keepdims=True)
        starts = starts + jnp.where(lane == j, count, 0.0)
        ends = ends + jnp.where(lane == j - 1, count, 0.0)

    def in_two(count):
        most = float(rows // 2)
        line = lax.broadcasted_iota(jnp.int32, (NOTE, HEAD), 0)
        low = jnp.minimum(count, most)
        return jnp.where(line == 0, low, jnp.where(line == 1, count - low, 0.0)).astype(jnp.bfloat16)

    def place(half, first, length):
        return pl.ds(pl.multiple_of(half * span + first, 16), length)

    kvs[z, place(core, rows, NOTE), 0:HEAD] = in_two(starts)
    kvs[z, place(core, rows, NOTE), HEAD:] = in_two(ends)

    def within(starts, ends):
        at = lax.broadcasted_iota(jnp.int32, (rows, HEAD), 0).astype(jnp.float32)
        return (at >= starts) & (at < ends)

    own_doc = jnp.where(within(starts[0:1, :], ends[0:1, :]), 1.0, 0.0).astype(jnp.bfloat16)
    for h in range(heads):
        qa[h * rows : (h + 1) * rows, HEAD:] = own_doc
    recv_kv[0] = kv_in[targets[0]]
    recv_q[0] = q_in[targets[0]]

    for step in range(1, reps):
        exchange(step, 0, send_kv, recv_kv).wait_recv()
    slots = [source_slot(b) for b in range(blocks)]
    for b in range(blocks):
        kvs[z, place(core, b * BLOCK, BLOCK), :] = recv_kv[slots[b]]

    def hop(slot, half, part, device, send, recv, k):
        where = kvs.at[slot, place(half, *pieces[part]), :]
        return pltpu.make_async_remote_copy(
            src_ref=where, dst_ref=where, send_sem=send.at[k, part], recv_sem=recv.at[k, part],
            device_id=device, device_id_type=MESH,
        )

    def up(slot, part, k):
        return hop(slot, core, part, above, up_send, up_recv, k)

    def far(slot, part, device):
        return hop(slot, core, part, device, far_send, far_recv, slot)

    def sib(slot, part, k):
        return hop(slot, core, part, sibling, sib_send, sib_recv, k)

    def from_sib(slot, k):
        for part in range(PARTS):
            hop(slot, 1 - core, part, sibling, sib_send, sib_recv, k).wait_recv()

    @pl.when(z < last)
    def _():
        pl.semaphore_wait(ready.at[0], 1)
        for part in range(PARTS):
            up(z, part, 1).start()

    @pl.when((z == 1) | (z == 2))
    def _():
        for part in range(PARTS):
            far(z, part, on_chip(0)).start()

    @pl.when(core == 0)
    def _():
        for part in range(PARTS):
            sib(z, part, 0).start()

    def has_far(k):
        first = (k == 2) & (z >= last - 1)
        second = ((k == 3) & (z == last)) | ((k == 4) & ((z == last - 1) | (z == last - 2)))
        return first | second

    def far_number(k):
        return jnp.where(k == 2, 1, 2)

    def far_slot(k):
        return jnp.maximum(z - last + far_number(k), 0)

    def take_up(k):
        slot = (z + chips - k) % chips

        @pl.when(z >= k)
        def _():
            for part in range(PARTS):
                up(slot, part, k).wait_recv()

                @pl.when((k < UP) & (z < last))
                def _():
                    up(slot, part, k + 1).start()

                sib(slot, part, k).start()

    def take_far(k):
        for part in range(PARTS):
            far(far_slot(k), part, below).wait_recv()

            @pl.when(k == 2)
            def _():
                far(far_slot(k), part, below).start()

            sib(far_slot(k), part, UP + far_number(k)).start()

    take_up(1)

    @pl.when(z == 0)
    def _():
        pl.semaphore_wait(ready.at[1], 1)
        for part in range(PARTS):
            far(0, part, on_chip(last - 1)).start()
        pl.semaphore_wait(ready.at[2], 1)
        for slot in (1, 2):
            for part in range(PARTS):
                far(slot, part, on_chip(last)).wait_recv()
                far(slot, part, on_chip(last)).start()

    for step in range(1, reps):
        exchange(step, 1, send_q, recv_q).wait_recv()
    for b in range(blocks):
        q_block = recv_q[slots[b]]
        for h in range(heads):
            qa[h * rows + b * BLOCK : h * rows + (b + 1) * BLOCK, 0:HEAD] = q_block[:, h * HEAD : (h + 1) * HEAD]

    def unit(slot, halves, diagonal):
        key_rows, value_rows = [], []
        for half in halves:
            note = kvs[slot, place(half, rows, NOTE), :].astype(jnp.float32)
            note = note[0:1, :] + note[1:2, :]
            hide = jnp.where(within(note[:, 0:HEAD], note[:, HEAD:]), 0.0, HIDE).astype(jnp.bfloat16)
            keys = kvs[slot, place(half, 0, rows), 0:HEAD]
            values = kvs[slot, place(half, 0, rows), HEAD:]
            key_rows.append(jnp.concatenate([keys, hide], axis=1))
            value_rows.append(jnp.concatenate([values, jnp.ones_like(values)], axis=1))
        key_rows = jnp.concatenate(key_rows, axis=0)
        value_rows = jnp.concatenate(value_rows, axis=0)

        def score(h):
            s = lax.dot_general(
                qa[h * rows : (h + 1) * rows, :], key_rows, (((1,), (1,)), ((), ())),
                preferred_element_type=jnp.float32,
            )
            if diagonal:
                ahead = lax.broadcasted_iota(jnp.int32, s.shape, 1) > lax.broadcasted_iota(jnp.int32, s.shape, 0)
                s = jnp.where(ahead, HIDE, s)
            return s

        def soften(h, s):
            part = slice(h * rows, (h + 1) * rows)
            high = jnp.max(s, axis=1, keepdims=True)
            if diagonal:
                now = jnp.broadcast_to(high, (rows, HEAD))
                decay = None
            else:
                now = jnp.maximum(top[part, :], high)
                decay = jnp.exp2((top[part, :] - now) * SCALE)
            top[part, :] = now
            p = jnp.exp2((s - jnp.concatenate([now] * (s.shape[1] // HEAD), axis=1)) * SCALE)
            return p.astype(jnp.bfloat16), decay

        def mix(h, p, decay):
            part = slice(h * rows, (h + 1) * rows)
            o = jnp.dot(p, value_rows, preferred_element_type=jnp.float32)
            if diagonal:
                acc[part, :] = o
            else:
                acc[part, :] = acc[part, :] * jnp.concatenate([decay] * 2, axis=1) + o

        scores = {0: score(0)}
        soft = {}
        for h in range(heads + 1):
            if h + 1 < heads:
                scores[h + 1] = score(h + 1)
            if h < heads:
                soft[h] = soften(h, scores.pop(h))
            if h >= 1:
                mix(h - 1, *soft.pop(h - 1))

    unit(z, [core], True)

    @pl.when(core == 1)
    def _():
        from_sib(z, 0)
        unit(z, [0], False)

    def receive(k, _):
        @pl.when(has_far(k))
        def _():
            take_far(k)

        @pl.when(z >= k)
        def _():
            slot = (z + chips - k) % chips
            from_sib(slot, k)
            unit(slot, [0, 1], False)

        @pl.when(k < UP)
        def _():
            take_up(k + 1)

        @pl.when(has_far(k))
        def _():
            from_sib(far_slot(k), UP + far_number(k))
            unit(far_slot(k), [0, 1], False)

        return 0

    lax.fori_loop(1, UP + 1, receive, 0)

    results = []
    for h in range(heads):
        part = slice(h * rows, (h + 1) * rows)
        columns = slice(h * HEAD, (h + 1) * HEAD)
        out[:, columns] = (acc[part, 0:HEAD] / acc[part, HEAD:]).astype(jnp.bfloat16)
        results.append(pltpu.make_async_copy(out.at[:, columns], out_hbm.at[0, :, columns], out_sem.at[h]))
        results[h].start()

    for step in range(1, reps):
        exchange(step, 0, send_kv, recv_kv).wait_send()
        exchange(step, 1, send_q, recv_q).wait_send()

    def drain(k, _):
        slot = (z + chips - k) % chips
        for part in range(PARTS):
            @pl.when(z >= k)
            def _():
                @pl.when((k < UP) & (z < last))
                def _():
                    up(slot, part, k + 1).wait_send()

                sib(slot, part, k).wait_send()

            @pl.when(has_far(k))
            def _():
                @pl.when(k == 2)
                def _():
                    far(far_slot(k), part, below).wait_send()

                sib(far_slot(k), part, UP + far_number(k)).wait_send()

        return 0

    lax.fori_loop(1, UP + 1, drain, 0)
    for part in range(PARTS):
        @pl.when(z < last)
        def _():
            up(z, part, 1).wait_send()

        @pl.when((z == 1) | (z == 2))
        def _():
            far(z, part, on_chip(0)).wait_send()

        @pl.when(z == 0)
        def _():
            for slot in range(3):
                far(slot, part, on_chip(last)).wait_send()

        @pl.when(core == 0)
        def _():
            sib(z, part, 0).wait_send()

    for result in results:
        result.wait()


def body(q_arrived, key_value_landed, finish, document_numbers):
    rows, q_width = q_arrived.shape[1:]
    kv_width = key_value_landed.shape[2]
    reps = lax.axis_size("rep")
    ctxs = lax.axis_size("ctx")
    heads = q_width // HEAD
    blocks = rows // BLOCK
    bf16, f32 = jnp.bfloat16, jnp.float32
    dma = pltpu.SemaphoreType.DMA
    return pl.pallas_call(
        functools.partial(kernel, reps, ctxs),
        out_shape=jax.ShapeDtypeStruct(q_arrived.shape, bf16),
        in_specs=[pl.BlockSpec(memory_space=pl.ANY)] * 4,
        out_specs=pl.BlockSpec(memory_space=pl.ANY),
        scratch_shapes=[
            pltpu.VMEM((blocks, BLOCK, q_width), bf16),
            pltpu.VMEM((blocks, BLOCK, kv_width), bf16),
            pltpu.SMEM(finish.shape, jnp.int32),
            pltpu.VMEM(document_numbers.shape, jnp.int32),
            pltpu.VMEM((reps, BLOCK, kv_width), bf16),
            pltpu.VMEM((reps, BLOCK, q_width), bf16),
            pltpu.VMEM((reps, BLOCK, kv_width), bf16),
            pltpu.VMEM((reps, BLOCK, q_width), bf16),
            pltpu.VMEM((ctxs // 2, 2 * (rows + NOTE), kv_width), bf16),
            pltpu.VMEM((heads * rows, 2 * HEAD), bf16),
            pltpu.VMEM((heads * rows, HEAD), f32),
            pltpu.VMEM((heads * rows, 2 * HEAD), f32),
            pltpu.VMEM((rows, q_width), bf16),
            dma((4,)),
            dma((2, reps)),
            dma((2, reps)),
            pltpu.SemaphoreType.REGULAR((3,)),
            dma((UP + 1, PARTS)),
            dma((UP + 1, PARTS)),
            dma((3, PARTS)),
            dma((3, PARTS)),
            dma((UP + 3, PARTS)),
            dma((UP + 3, PARTS)),
            dma((heads,)),
        ],
        compiler_params=pltpu.CompilerParams(
            collective_id=0, has_side_effects=True, vmem_limit_bytes=62 * 2**20
        ),
    )(
        q_arrived.reshape(blocks, BLOCK, q_width),
        key_value_landed.reshape(blocks, BLOCK, kv_width),
        finish,
        document_numbers,
    )


def solution(mesh):
    in_specs = (P("rep", "ctx", "tp"), P("rep", "ctx", "tp"), P("ctx", None), P("rep", "ctx"))
    out_specs = P("rep", "ctx", "tp")
    return jax.shard_map(body, mesh=mesh, in_specs=in_specs, out_specs=out_specs, check_vma=False)
```
